256 devices in a mesh: vocab: 32 (over y, z), rows: 8 (over x, core).
Axes of the slice: x: 4, y: 4, z: 8, core: 2. Of those that a mesh axis runs over, the one named last changes fastest.
Arguments:
- hidden_states: bfloat16 [512, 5120], P(('vocab', 'rows')), may hold values from -1000 to 1000
- head_weight: bfloat16 [151552, 5120], P(('vocab', 'rows')), may hold values from -2 to 2
- teacher_ids: int32 [512, 64], P(('vocab', 'rows')), may hold values from 0 to 151551
- teacher_probs: float32 [512, 64], P(('vocab', 'rows')), may hold values from 0.001 to 0.015
- row_weight: float32 [512], P(('vocab', 'rows')), may hold values from 16 to 160
Outputs:
- grad_hidden: bfloat16 [512, 5120], P(('vocab', 'rows'))
- grad_weight: bfloat16 [151552, 5120], P(('vocab', 'rows'))
The draws below stay inside these ranges and needn't reach their ends.
All inputs are finite; a program needn't handle non-finite values.
Results may differ from the reference program's by a relative error of at most 0.012.
Values may be sent and summed in bfloat16 or wider, within the bound.
No kernel may reach another device: no remote copies, remote signals or barrier semaphores. Data moves between devices by JAX's collectives and lax.ppermute only.
A program may use at most 128 MiB of HBM per device.

```python
import math
import jax
import jax.numpy as jnp
import numpy as np

D = 5120
VOCAB = 151552
K = 64
ROWS = 512


def weight_row(key, row_number):
    source = jax.random.fold_in(jax.random.fold_in(key, 11), row_number)
    values = jnp.clip(jax.random.normal(source, (D,), jnp.float32), -6.0, 6.0)
    return values * (2.0 / math.sqrt(D))


def draw_head_weight(key, part):
    numbers = jnp.arange(VOCAB, dtype=jnp.int32)
    return jax.vmap(lambda row_number: weight_row(key, row_number))(numbers).astype(jnp.bfloat16)


def draw_hidden_states(key, part):
    own_key = jax.random.fold_in(key, 7)
    result = jnp.clip(jax.random.normal(own_key, (ROWS, D), jnp.float32), -6.0, 6.0) * 1.5
    return result.astype(jnp.bfloat16)


def with_ends(values, key, low, top_value):
    longest = values.shape.index(max(values.shape))
    spots = []
    for shift in (0, 1):
        where = [jax.random.randint(jax.random.fold_in(key, axis), (), 0, length) for axis, length in enumerate(values.shape)]
        where[longest] = (where[longest] + shift) % values.shape[longest]
        spots.append(tuple(where))
    return values.at[spots[0]].set(low).at[spots[1]].set(top_value)


def level_of(rng, dims, pieces, least, top_value):
    gain = 1.0
    for position, blocks in pieces:
        draws = jax.random.uniform(jax.random.fold_in(jax.random.fold_in(rng, 6), position), (blocks,), jnp.float32, least / len(pieces), top_value / len(pieces))
        gain = gain * jnp.repeat(jnp.exp(draws), dims[position] // blocks).reshape((-1,) + (1,) * (len(dims) - 1 - position))
    return gain


def wide_ids(rng, dims, count, skew):
    portions = [min(1 << octave, count + 1 - (1 << octave)) * (1 << 20) // math.isqrt((1 << octave) ** skew) + 1 for octave in range((count + 1).bit_length()) if 1 << octave <= count]
    spread = 1 + sum(portions) // (1 << 30)
    table = np.cumsum(np.array([max(1, weight // spread) for weight in portions]))
    lot = jax.random.randint(jax.random.fold_in(rng, 1), dims, 0, int(table[len(portions) - 1]))
    start = jnp.left_shift(1, jnp.searchsorted(jnp.asarray(table, jnp.int32), lot, side="right").astype(jnp.int32))
    grade = start - 1 + jax.random.randint(jax.random.fold_in(rng, 4), dims, 0, 1 << 30) % jnp.minimum(start, count + 1 - start)
    return jax.random.permutation(jax.random.fold_in(rng, 2), count)[grade].astype(jnp.int32)


def setup_inputs(seed: int = 0) -> dict:
    arg_keys = jax.random.split(jax.random.key(seed), 6)
    hidden_states = draw_hidden_states(jax.random.fold_in(arg_keys[5], 71), 0)
    head_weight = draw_head_weight(jax.random.fold_in(arg_keys[5], 71), 0)
    teacher_ids = with_ends(wide_ids(arg_keys[2], (ROWS, K), VOCAB, 2), jax.random.fold_in(arg_keys[2], 3), 0, VOCAB - 1).astype(jnp.int32)
    teacher_probs = jnp.clip(jnp.exp(math.log(0.015) - 2.70805 * jax.random.uniform(arg_keys[3], (ROWS, K), jnp.float32) ** level_of(arg_keys[3], (ROWS, K), ((0, 256),), -0.2, 0.2)), 0.001, 0.015)
    row_weight = jnp.clip(jnp.exp(math.log(160.0) - 2.3025851 * jax.random.uniform(arg_keys[4], (ROWS,), jnp.float32) ** level_of(arg_keys[4], (ROWS,), ((0, 256),), -0.2, 0.2)), 16.0, 160.0)
    return {"hidden_states": hidden_states, "head_weight": head_weight, "teacher_ids": teacher_ids, "teacher_probs": teacher_probs, "row_weight": row_weight}


def reference(hidden_states, head_weight, teacher_ids, teacher_probs, row_weight):
    logits = jnp.dot(hidden_states, head_weight.T, preferred_element_type=jnp.float32)
    row_top = jnp.max(logits, axis=1, keepdims=True)
    exponent = jnp.exp(logits - row_top)
    row_total = jnp.sum(exponent, axis=1, keepdims=True)
    row_index = jnp.broadcast_to(jnp.arange(ROWS, dtype=jnp.int32)[:, None], teacher_ids.shape)
    target = jnp.zeros(logits.shape, jnp.float32).at[row_index, teacher_ids].add(teacher_probs)
    teacher_mass = jnp.sum(teacher_probs, axis=1, keepdims=True)
    grad_logits = (row_weight[:, None] * (teacher_mass * exponent / row_total - target)).astype(jnp.bfloat16)
    grad_hidden = jnp.dot(grad_logits, head_weight, preferred_element_type=jnp.float32).astype(jnp.bfloat16)
    grad_weight = jnp.dot(grad_logits.T, hidden_states, preferred_element_type=jnp.float32).astype(jnp.bfloat16)
    return grad_hidden, grad_weight
```

```python
import jax
import jax.numpy as jnp
from jax import lax
from jax.sharding import Mesh, PartitionSpec as P

AXES = ("y", "z", "x", "core")
SWAP = [(0, 1), (1, 0)]
DIGIT = 512
HALF = 256
ID_SHIFT = 148


def split_bf16(value, pieces):
    parts = []
    for _ in range(pieces):
        part = value.astype(jnp.bfloat16)
        parts.append(part)
        value = value - part.astype(jnp.float32)
    return parts


def spread(block, axes, count):
    copies = jnp.broadcast_to(block[None], (count,) + block.shape)
    return lax.all_to_all(copies, axes, 0, 0, tiled=True)


def dense_target(local_ids, weighted_probs, entries):
    columns = jnp.arange(entries, dtype=jnp.int32)
    matches = local_ids.T[:, None, :] == columns[None, :, None]
    return jnp.sum(jnp.where(matches, weighted_probs.T[:, None, :], jnp.float32(0.0)), axis=0)


def per_device(sizes, hidden_states, head_weight, teacher_ids, teacher_probs, row_weight):
    size_y, size_z, size_x, _ = sizes
    own_rows, width = hidden_states.shape
    entries = head_weight.shape[0]
    kept = teacher_ids.shape[1]
    other_weight = lax.ppermute(head_weight, "core", SWAP)

    with jax.named_scope("pack"):
        mass = row_weight * jnp.sum(teacher_probs, axis=1)
        weighted = row_weight[:, None] * teacher_probs
        high = teacher_ids // DIGIT - ID_SHIFT
        low = teacher_ids % DIGIT - HALF
        extra = [high.astype(jnp.bfloat16), low.astype(jnp.bfloat16)]
        extra += split_bf16(weighted, 2)
        extra += split_bf16(mass[:, None], 3)
        used = sum(piece.shape[1] for piece in extra)
        padding = -used % 128
        extra.append(jnp.zeros((own_rows, padding), jnp.bfloat16))
        packed = jnp.concatenate([hidden_states] + extra, axis=1)

    with jax.named_scope("gather"):
        across_z = spread(packed, "z", size_z).reshape(size_z * own_rows, -1)
        gathered = spread(across_z, ("y", "x"), size_y * size_x)
        rows = size_y * size_x * size_z * own_rows
        gathered = gathered.reshape(rows, -1)

    hidden = gathered[:, :width]
    with jax.named_scope("unpack"):
        tail = gathered[:, width:].astype(jnp.float32)
        high = tail[:, :kept].astype(jnp.int32) + ID_SHIFT
        low = tail[:, kept : 2 * kept].astype(jnp.int32) + HALF
        ids = high * DIGIT + low
        weighted = tail[:, 2 * kept : 3 * kept] + tail[:, 3 * kept : 4 * kept]
        mass = tail[:, 4 * kept] + tail[:, 4 * kept + 1] + tail[:, 4 * kept + 2]

    device = lax.axis_index(AXES)
    core = lax.axis_index("core")
    first = device * entries
    other_first = (device + 1 - 2 * core) * entries
    with jax.named_scope("target"):
        target = dense_target(ids - first, weighted, entries)
        other_target = dense_target(ids - other_first, weighted, entries)

    with jax.named_scope("logits"):
        logits = jnp.einsum("vd,rd->vr", head_weight, hidden, preferred_element_type=jnp.float32)
        other_logits = jnp.einsum(
            "vd,rd->vr", other_weight, hidden, preferred_element_type=jnp.float32
        )
        top = jnp.maximum(jnp.max(logits, axis=0), jnp.max(other_logits, axis=0))
        exponent = jnp.exp(logits - top[None])
        other_exponent = jnp.exp(other_logits - top[None])
        total = jnp.sum(exponent, axis=0) + jnp.sum(other_exponent, axis=0)

    with jax.named_scope("stats"):
        stats = spread(jnp.stack([top, total]), ("y", "z", "x"), size_y * size_z * size_x)
        stats = stats.reshape(-1, 2, rows)
        row_top = jnp.max(stats[:, 0], axis=0)
        row_total = jnp.sum(stats[:, 1] * jnp.exp(stats[:, 0] - row_top[None]), axis=0)
        scale = mass * jnp.exp(top - row_top) / row_total

    with jax.named_scope("grads"):
        grad = (exponent * scale[None] - target).astype(jnp.bfloat16)
        other_grad = (other_exponent * scale[None] - other_target).astype(jnp.bfloat16)
        other_part = jnp.dot(other_grad, hidden, preferred_element_type=jnp.float32)
        returned = lax.ppermute(other_part.astype(jnp.bfloat16), "core", SWAP)
        partial = jnp.einsum(
            "vr,vd->rd", grad, head_weight, preferred_element_type=jnp.float32
        ) + jnp.einsum("vr,vd->rd", other_grad, other_weight, preferred_element_type=jnp.float32)
        partial = partial.astype(jnp.bfloat16)

    with jax.named_scope("scatter"):
        pieces = partial.reshape(size_y * size_x, size_z * own_rows, width)
        pieces = lax.all_to_all(pieces, ("y", "x"), 0, 0, tiled=True)
        summed = jnp.sum(pieces.astype(jnp.float32), axis=0).astype(jnp.bfloat16)
        pieces = summed.reshape(size_z, own_rows, width)
        pieces = lax.all_to_all(pieces, "z", 0, 0, tiled=True)
        grad_hidden = jnp.sum(pieces.astype(jnp.float32), axis=0).astype(jnp.bfloat16)

    with jax.named_scope("grad_weight"):
        own_part = jnp.dot(grad, hidden, preferred_element_type=jnp.float32)
        grad_weight = (own_part + returned.astype(jnp.float32)).astype(jnp.bfloat16)
    return grad_hidden, grad_weight


def solution(mesh):
    sizes = (4, 8, 4, 2)
    grid = Mesh(mesh.devices.reshape(sizes), AXES)
    in_specs = (P(AXES, None), P(AXES, None), P(AXES, None), P(AXES, None), P(AXES))
    out_specs = (P(AXES, None), P(AXES, None))

    def body(*args):
        return per_device(sizes, *args)

    return jax.shard_map(
        body, mesh=grid, in_specs=in_specs, out_specs=out_specs, check_vma=False
    )
```

```python
import jax
import jax.numpy as jnp
import numpy as np
from jax import lax
from jax.sharding import Mesh, PartitionSpec as P

AXES = ("y", "z", "x", "core")
SWAP = [(0, 1), (1, 0)]
SIDE = 4
DIGIT = 512
HALF = 256
ID_SHIFT = 148


def split_bf16(value, pieces):
    parts = []
    for _ in range(pieces):
        part = value.astype(jnp.bfloat16)
        parts.append(part)
        value = value - part.astype(jnp.float32)
    return parts


def spread(block, axes, count):
    copies = jnp.broadcast_to(block[None], (count,) + block.shape)
    return lax.all_to_all(copies, axes, 0, 0, tiled=True)


def partner(block, sizes, leg, step):
    pairs = []
    for source, (y, z, x, core) in enumerate(np.ndindex(*sizes)):
        if (core + leg) % 2 == 0:
            x = x ^ step
        else:
            y = y ^ step
        pairs.append((source, int(np.ravel_multi_index((y, z, x, core), sizes))))
    return lax.ppermute(block, AXES, pairs)


def gather_blocks(block, sizes, leg, place):
    result = jnp.zeros((SIDE,) + block.shape, block.dtype)
    for step in range(SIDE):
        piece = partner(block, sizes, leg, step) if step else block
        result = lax.dynamic_update_index_in_dim(result, piece, place ^ step, 0)
    return result.reshape((-1,) + block.shape[1:])


def scatter_blocks(values, sizes, leg, place):
    values = values.reshape((SIDE, -1) + values.shape[1:])
    pieces = []
    for step in range(SIDE):
        piece = lax.dynamic_index_in_dim(values, place ^ step, 0, keepdims=False)
        pieces.append(partner(piece, sizes, leg, step) if step else piece)
    return pieces


def total(pieces):
    result = pieces[0].astype(jnp.float32)
    for piece in pieces[1:]:
        result = result + piece.astype(jnp.float32)
    return result.astype(jnp.bfloat16)


def dense_target(local_ids, weighted_probs, entries):
    columns = jnp.arange(entries, dtype=jnp.int32)
    matches = local_ids.T[:, None, :] == columns[None, :, None]
    return jnp.sum(jnp.where(matches, weighted_probs.T[:, None, :], jnp.float32(0.0)), axis=0)


def per_device(sizes, hidden_states, head_weight, teacher_ids, teacher_probs, row_weight):
    size_y, size_z, size_x, _ = sizes
    own_rows, width = hidden_states.shape
    entries = head_weight.shape[0]
    kept = teacher_ids.shape[1]
    group = size_z * own_rows
    rows = size_y * size_x * group
    core = lax.axis_index("core")
    place_x, place_y = lax.axis_index("x"), lax.axis_index("y")
    first_place = jnp.where(core == 0, place_x, place_y)
    second_place = jnp.where(core == 0, place_y, place_x)
    other_weight = lax.ppermute(head_weight, "core", SWAP)

    with jax.named_scope("pack"):
        mass = row_weight * jnp.sum(teacher_probs, axis=1)
        weighted = row_weight[:, None] * teacher_probs
        high = teacher_ids // DIGIT - ID_SHIFT
        low = teacher_ids % DIGIT - HALF
        extra = [high.astype(jnp.bfloat16), low.astype(jnp.bfloat16)]
        extra += split_bf16(weighted, 2)
        extra += split_bf16(mass[:, None], 3)
        used = sum(piece.shape[1] for piece in extra)
        tail_width = used + -used % 128
        extra.append(jnp.zeros((own_rows, tail_width - used), jnp.bfloat16))
        packed = jnp.concatenate(extra + [hidden_states], axis=1)

    with jax.named_scope("gather"):
        across_z = spread(packed, "z", size_z).reshape(group, -1)
        gathered = gather_blocks(across_z, sizes, 0, first_place)
        gathered = gather_blocks(gathered, sizes, 1, second_place)
        hidden = gathered[:, tail_width:]

    with jax.named_scope("unpack"):
        tail = gathered[:, :tail_width].astype(jnp.float32)
        high = tail[:, :kept].astype(jnp.int32) + ID_SHIFT
        low = tail[:, kept : 2 * kept].astype(jnp.int32) + HALF
        ids = high * DIGIT + low
        weighted = tail[:, 2 * kept : 3 * kept] + tail[:, 3 * kept : 4 * kept]
        mass = tail[:, 4 * kept] + tail[:, 4 * kept + 1] + tail[:, 4 * kept + 2]

    device = lax.axis_index(AXES)
    first = device * entries
    other_first = (device + 1 - 2 * core) * entries
    with jax.named_scope("target"):
        target = dense_target(ids - first, weighted, entries)
        other_target = dense_target(ids - other_first, weighted, entries)

    with jax.named_scope("logits"):
        logits = jnp.einsum("vd,rd->vr", head_weight, hidden, preferred_element_type=jnp.float32)
        other_logits = jnp.einsum(
            "vd,rd->vr", other_weight, hidden, preferred_element_type=jnp.float32
        )
        top = jnp.maximum(jnp.max(logits, axis=0), jnp.max(other_logits, axis=0))
        exponent = jnp.exp(logits - top[None])
        other_exponent = jnp.exp(other_logits - top[None])
        row_sum = jnp.sum(exponent, axis=0) + jnp.sum(other_exponent, axis=0)

    with jax.named_scope("stats"):
        stats = spread(jnp.stack([top, row_sum]), ("y", "z", "x"), size_y * size_z * size_x)
        stats = stats.reshape(-1, 2, rows)
        row_top = jnp.max(stats[:, 0], axis=0)
        row_total = jnp.sum(stats[:, 1] * jnp.exp(stats[:, 0] - row_top[None]), axis=0)
        scale = mass * jnp.exp(top - row_top) / row_total

    with jax.named_scope("grads"):
        grad = (exponent * scale[None] - target).astype(jnp.bfloat16)
        other_grad = (other_exponent * scale[None] - other_target).astype(jnp.bfloat16)
        partial = jnp.einsum(
            "vr,vd->rd", grad, head_weight, preferred_element_type=jnp.float32
        ) + jnp.einsum("vr,vd->rd", other_grad, other_weight, preferred_element_type=jnp.float32)
        partial = partial.astype(jnp.bfloat16)

    with jax.named_scope("scatter"):
        partial, other_grad = lax.optimization_barrier((partial, other_grad))
        pieces = scatter_blocks(partial, sizes, 1, second_place)

    with jax.named_scope("grad_weight"):
        other_part = jnp.dot(other_grad, hidden, preferred_element_type=jnp.float32)
        other_part = other_part.astype(jnp.bfloat16)
        returned = lax.ppermute(other_part, "core", SWAP)

    with jax.named_scope("scatter"):
        pieces[0], other_part = lax.optimization_barrier((pieces[0], other_part))
        summed = total(pieces)
        summed, grad = lax.optimization_barrier((summed, grad))
        pieces = scatter_blocks(summed, sizes, 0, first_place)

    with jax.named_scope("grad_weight"):
        own_part = jnp.dot(grad, hidden, preferred_element_type=jnp.float32)
        grad_weight = (own_part + returned.astype(jnp.float32)).astype(jnp.bfloat16)

    with jax.named_scope("scatter"):
        pieces[0], grad_weight = lax.optimization_barrier((pieces[0], grad_weight))
        summed = total(pieces).reshape(size_z, own_rows, width)
        pieces = lax.all_to_all(summed, "z", 0, 0, tiled=True)
        grad_hidden = jnp.sum(pieces.astype(jnp.float32), axis=0).astype(jnp.bfloat16)
    return grad_hidden, grad_weight


def solution(mesh):
    sizes = (4, 8, 4, 2)
    grid = Mesh(mesh.devices.reshape(sizes), AXES)
    in_specs = (P(AXES, None), P(AXES, None), P(AXES, None), P(AXES, None), P(AXES))
    out_specs = (P(AXES, None), P(AXES, None))

    def body(*args):
        return per_device(sizes, *args)

    return jax.shard_map(
        body, mesh=grid, in_specs=in_specs, out_specs=out_specs, check_vma=False
    )
```

```python
import jax
import jax.numpy as jnp
import numpy as np
from jax import lax
from jax.experimental import pallas as pl
from jax.experimental.pallas import tpu as pltpu
from jax.sharding import Mesh, PartitionSpec as P

AXES = ("y", "z", "x", "core")
SWAP = [(0, 1), (1, 0)]
SIDE = 4
DIGIT = 512
HALF = 256
ID_SHIFT = 148


def spread(block, axes, count):
    copies = jnp.broadcast_to(block[None], (count,) + block.shape)
    return lax.all_to_all(copies, axes, 0, 0, tiled=True)


def partner(block, sizes, leg, step):
    pairs = []
    for source, (y, z, x, core) in enumerate(np.ndindex(*sizes)):
        if (core + leg) % 2 == 0:
            x = x ^ step
        else:
            y = y ^ step
        pairs.append((source, int(np.ravel_multi_index((y, z, x, core), sizes))))
    return lax.ppermute(block, AXES, pairs)


def gather_blocks(block, sizes, leg, spots):
    result = jnp.zeros((SIDE,) + block.shape, block.dtype)
    for step in range(SIDE):
        piece = partner(block, sizes, leg, step) if step else block
        result = lax.dynamic_update_slice(
            result, piece[None], (spots[step],) + (jnp.uint32(0),) * block.ndim
        )
    return result.reshape((-1,) + block.shape[1:])


def scatter_blocks(values, sizes, leg, spots):
    values = values.reshape((SIDE, -1) + values.shape[1:])
    pieces = []
    for step in range(SIDE):
        start = (spots[step],) + (jnp.uint32(0),) * (values.ndim - 1)
        piece = lax.dynamic_slice(values, start, (1,) + values.shape[1:])[0]
        pieces.append(partner(piece, sizes, leg, step) if step else piece)
    return pieces


def total(pieces):
    result = pieces[0].astype(jnp.float32)
    for piece in pieces[1:]:
        result = result + piece.astype(jnp.float32)
    return result.astype(jnp.bfloat16)


def rounded(value):
    return value.astype(jnp.bfloat16).astype(jnp.float32)


def pack_kernel(weight_ref, hidden_ref, ids_ref, probs_ref, out_ref):
    probs = probs_ref[...]
    own_rows, kept = probs.shape
    width = hidden_ref.shape[1]
    row = lax.broadcasted_iota(jnp.int32, (own_rows, 1), 0)
    weight = jnp.zeros((own_rows, 1), jnp.float32)
    for i in range(own_rows):
        weight = jnp.where(row == i, weight_ref[i], weight)
    ids = ids_ref[...]
    high = ((ids >> 9) - ID_SHIFT).astype(jnp.float32)
    low = ((ids & (DIGIT - 1)) - HALF).astype(jnp.float32)
    weighted = probs * weight
    weighted_high = rounded(weighted)
    mass = jnp.sum(probs, axis=1, keepdims=True) * weight
    column = lax.broadcasted_iota(jnp.int32, (own_rows, 2 * kept), 1)
    pieces = jnp.zeros((own_rows, 2 * kept), jnp.float32)
    for i in range(3):
        part = rounded(mass)
        pieces = jnp.where(column == i, part, pieces)
        mass = mass - part
    tail = jnp.concatenate(
        [
            jnp.concatenate([high, low], axis=1),
            jnp.concatenate([weighted_high, rounded(weighted - weighted_high)], axis=1),
            pieces,
        ],
        axis=1,
    ).astype(jnp.bfloat16)
    hidden = hidden_ref[...]
    for i in range(out_ref.shape[0]):
        out_ref[i, :, :width] = hidden
        out_ref[i, :, width:] = tail


def pack(hidden, ids, probs, weight, copies):
    own_rows, width = hidden.shape
    kept = ids.shape[1]
    vmem = pl.BlockSpec(memory_space=pltpu.VMEM)
    return pl.pallas_call(
        pack_kernel,
        out_shape=jax.ShapeDtypeStruct((copies, own_rows, width + 6 * kept), jnp.bfloat16),
        in_specs=[pl.BlockSpec(memory_space=pltpu.SMEM), vmem, vmem, vmem],
        out_specs=vmem,
        name="pack",
    )(weight, hidden, ids, probs)


def target_kernel(first_ref, digits_ref, probs_ref, out_ref, place_ref):
    entries = out_ref.shape[0] // 2
    kept = place_ref.shape[0]
    digits = digits_ref[...].astype(jnp.float32).T.astype(jnp.int32)
    probs = probs_ref[...].astype(jnp.float32).T
    probs = probs[:kept] + probs[kept:]
    ids = (digits[:kept] + ID_SHIFT) * DIGIT + digits[kept:] + HALF
    own = ids - first_ref[0]
    other = ids - first_ref[1]
    none = jnp.int32(4 * entries)
    place = jnp.where((other >= 0) & (other < entries), other + entries, none)
    place = jnp.where((own >= 0) & (own < entries), own, place)
    place_ref[...] = place
    out_ref[...] = jnp.zeros_like(out_ref)
    rows = out_ref.shape[1]
    step = 16
    index = lax.broadcasted_iota(jnp.int32, (step, rows), 0)

    def body(lowest):
        place = place_ref[...]
        chosen = jnp.min(place, axis=0, keepdims=True)
        hit = place == chosen
        amount = jnp.sum(jnp.where(hit, probs, 0.0), axis=0, keepdims=True)
        rest = jnp.where(hit, none, place)
        place_ref[...] = rest

        def one(i, carry):
            at = pl.ds(pl.multiple_of(i * step, step), step)
            out_ref[at] = jnp.where(index + i * step == chosen, amount, out_ref[at])
            return carry

        lax.fori_loop(0, 2 * entries // step, one, 0, unroll=2)
        return jnp.min(rest)

    lax.while_loop(lambda lowest: lowest < none, body, jnp.min(place))


def dense_target(gathered, firsts, width, kept, entries):
    rows = gathered.shape[0]
    at = width // (2 * kept)
    return pl.pallas_call(
        target_kernel,
        out_shape=jax.ShapeDtypeStruct((2 * entries, rows), jnp.float32),
        grid=(1,),
        in_specs=[
            pl.BlockSpec(memory_space=pltpu.SMEM),
            pl.BlockSpec((rows, 2 * kept), lambda i: (0, at)),
            pl.BlockSpec((rows, 2 * kept), lambda i: (0, at + 1)),
        ],
        out_specs=pl.BlockSpec((2 * entries, rows), lambda i: (0, 0)),
        scratch_shapes=[pltpu.VMEM((kept, rows), jnp.int32)],
        cost_estimate=pl.CostEstimate(flops=10000000, bytes_accessed=4000000, transcendentals=0),
        compiler_params=pltpu.CompilerParams(vmem_limit_bytes=8 * 1024 * 1024),
        name="target",
    )(firsts, gathered, gathered)


def logits_kernel(gathered_ref, own_ref, other_ref, exp_ref, stats_ref):
    entries, width = own_ref.shape
    tile = 1024
    dims = (((1,), (1,)), ((), ()))
    for start in range(0, width, tile):
        at = slice(start, start + tile)
        hidden = gathered_ref[:, at]
        for i, ref in enumerate((own_ref, other_ref)):
            part = lax.dot_general(ref[:, at], hidden, dims, preferred_element_type=jnp.float32)
            rows = slice(i * entries, (i + 1) * entries)
            exp_ref[rows] = part if start == 0 else exp_ref[rows] + part
    logits = exp_ref[...]
    top = jnp.max(logits, axis=0, keepdims=True)
    exponent = jnp.exp(logits - top)
    exp_ref[...] = exponent
    stats_ref[0:1] = top
    stats_ref[1:2] = jnp.sum(exponent, axis=0, keepdims=True)


def exponents(gathered, own_weight, other_weight):
    rows = gathered.shape[0]
    entries, width = own_weight.shape
    vmem = pl.BlockSpec(memory_space=pltpu.VMEM)
    return pl.pallas_call(
        logits_kernel,
        out_shape=(
            jax.ShapeDtypeStruct((2 * entries, rows), jnp.float32),
            jax.ShapeDtypeStruct((2, rows), jnp.float32),
        ),
        in_specs=[vmem] * 3,
        out_specs=(vmem, vmem),
        compiler_params=pltpu.CompilerParams(vmem_limit_bytes=24 * 1024 * 1024),
        cost_estimate=pl.CostEstimate(
            flops=4 * entries * rows * width,
            bytes_accessed=4 * entries * width,
            transcendentals=2 * entries * rows,
        ),
        name="exponents",
    )(gathered, own_weight, other_weight)


def grad_kernel(
    stats_ref, local_ref, gathered_ref, exp_ref, target_ref, own_ref, other_ref,
    out_ref, own_grad_ref, other_grad_ref,
):
    entries, width = own_ref.shape
    tile = 512
    tops = stats_ref[:, 0, :]
    top = jnp.max(tops, axis=0, keepdims=True)
    total = jnp.sum(stats_ref[:, 1, :] * jnp.exp(tops - top), axis=0, keepdims=True)
    tail = gathered_ref[:, gathered_ref.shape[1] - 128 :]
    mass = jnp.sum(tail.astype(jnp.float32).T, axis=0, keepdims=True)
    scale = mass * jnp.exp(local_ref[0:1] - top) / total
    grad = (exp_ref[...] * scale - target_ref[...]).astype(jnp.bfloat16)
    own_grad_ref[...] = grad[:entries]
    other_grad_ref[...] = grad[entries:]
    own_turned = grad[:entries].T
    other_turned = grad[entries:].T
    for start in range(0, width, tile):
        at = slice(start, start + tile)
        out = jnp.dot(own_turned, own_ref[:, at], preferred_element_type=jnp.float32)
        out += jnp.dot(other_turned, other_ref[:, at], preferred_element_type=jnp.float32)
        out_ref[:, at] = out.astype(jnp.bfloat16)


def gradients(stats, local, gathered, exponent, target, own_weight, other_weight, kept):
    entries, width = own_weight.shape
    rows = gathered.shape[0]
    vmem = pl.BlockSpec(memory_space=pltpu.VMEM)
    return pl.pallas_call(
        grad_kernel,
        out_shape=(
            jax.ShapeDtypeStruct((rows, width), jnp.bfloat16),
            jax.ShapeDtypeStruct((entries, rows), jnp.bfloat16),
            jax.ShapeDtypeStruct((entries, rows), jnp.bfloat16),
        ),
        in_specs=[vmem] * 7,
        out_specs=(vmem,) * 3,
        compiler_params=pltpu.CompilerParams(vmem_limit_bytes=28 * 1024 * 1024),
        cost_estimate=pl.CostEstimate(
            flops=4 * entries * rows * width,
            bytes_accessed=4 * entries * width,
            transcendentals=0,
        ),
        name="gradients",
    )(stats, local, gathered, exponent, target, own_weight, other_weight)


def per_device(sizes, hidden_states, head_weight, teacher_ids, teacher_probs, row_weight):
    size_y, size_z, size_x, _ = sizes
    own_rows, width = hidden_states.shape
    entries = head_weight.shape[0]
    kept = teacher_ids.shape[1]
    group = size_z * own_rows
    rows = size_y * size_x * group
    core = lax.axis_index("core")
    device = lax.axis_index(AXES)
    place_x, place_y = lax.axis_index("x"), lax.axis_index("y")
    first_place = jnp.where(core == 0, place_x, place_y).astype(jnp.uint32)
    second_place = jnp.where(core == 0, place_y, place_x).astype(jnp.uint32)
    first_spots = [first_place ^ step for step in range(SIDE)]
    second_spots = [second_place ^ step for step in range(SIDE)]
    firsts = jnp.stack([device * entries, (device + 1 - 2 * core) * entries])
    other_weight = lax.ppermute(head_weight, "core", SWAP)

    with jax.named_scope("pack"):
        hidden_states, first_spots, second_spots, firsts = lax.optimization_barrier(
            (hidden_states, first_spots, second_spots, firsts)
        )
        packed = pack(hidden_states, teacher_ids, teacher_probs, row_weight, size_z)

    with jax.named_scope("gather"):
        across_z = lax.all_to_all(packed, "z", 0, 0, tiled=True).reshape(group, -1)
        gathered = gather_blocks(across_z, sizes, 0, first_spots)
        gathered = gather_blocks(gathered, sizes, 1, second_spots)
        hidden = gathered[:, :width]

    with jax.named_scope("target"):
        target = dense_target(gathered, firsts, width, kept, entries)

    with jax.named_scope("logits"):
        exponent, local = exponents(gathered, head_weight, other_weight)

    with jax.named_scope("stats"):
        local, target = lax.optimization_barrier((local, target))
        stats = spread(local, ("y", "z", "x"), size_y * size_z * size_x)
        stats = stats.reshape(-1, 2, rows)

    with jax.named_scope("grads"):
        partial, grad, other_grad = gradients(
            stats, local, gathered, exponent, target, head_weight, other_weight, kept
        )

    with jax.named_scope("scatter"):
        partial, other_grad = lax.optimization_barrier((partial, other_grad))
        pieces = scatter_blocks(partial, sizes, 1, second_spots)

    with jax.named_scope("grad_weight"):
        other_part = jnp.dot(other_grad, hidden, preferred_element_type=jnp.float32)
        other_part = other_part.astype(jnp.bfloat16)
        returned = lax.ppermute(other_part, "core", SWAP)

    with jax.named_scope("scatter"):
        pieces[0], other_part = lax.optimization_barrier((pieces[0], other_part))
        summed = total(pieces)
        summed, grad = lax.optimization_barrier((summed, grad))
        pieces = scatter_blocks(summed, sizes, 0, first_spots)

    with jax.named_scope("grad_weight"):
        own_part = jnp.dot(grad, hidden, preferred_element_type=jnp.float32)
        grad_weight = (own_part + returned.astype(jnp.float32)).astype(jnp.bfloat16)

    with jax.named_scope("scatter"):
        pieces[0], grad_weight = lax.optimization_barrier((pieces[0], grad_weight))
        summed = total(pieces).reshape(size_z, own_rows, width)
        pieces = lax.all_to_all(summed, "z", 0, 0, tiled=True)
        grad_hidden = jnp.sum(pieces.astype(jnp.float32), axis=0).astype(jnp.bfloat16)
    return grad_hidden, grad_weight


def solution(mesh):
    sizes = (4, 8, 4, 2)
    grid = Mesh(mesh.devices.reshape(sizes), AXES)
    in_specs = (P(AXES, None), P(AXES, None), P(AXES, None), P(AXES, None), P(AXES))
    out_specs = (P(AXES, None), P(AXES, None))

    def body(*args):
        return per_device(sizes, *args)

    return jax.shard_map(
        body, mesh=grid, in_specs=in_specs, out_specs=out_specs, check_vma=False
    )
```

```python
import jax
import jax.numpy as jnp
import numpy as np
from jax import lax
from jax.experimental import pallas as pl
from jax.experimental.pallas import tpu as pltpu
from jax.sharding import Mesh, PartitionSpec as P

AXES = ("y", "z", "x", "core")
SWAP = [(0, 1), (1, 0)]
SIDE = 4
STEPS = (0, 2, 1, 3)
DIGIT = 512
HALF = 256
ID_SHIFT = 148


def spread(block, axes, count):
    copies = jnp.broadcast_to(block[None], (count,) + block.shape)
    return lax.all_to_all(copies, axes, 0, 0, tiled=True)


def partner(block, sizes, leg, step):
    pairs = []
    for source, (y, z, x, core) in enumerate(np.ndindex(*sizes)):
        if (core + leg) % 2 == 0:
            x = x ^ step
        else:
            y = y ^ step
        pairs.append((source, int(np.ravel_multi_index((y, z, x, core), sizes))))
    return lax.ppermute(block, AXES, pairs)


def gather_blocks(block, sizes, leg, spots, beside=None):
    own = block
    if beside is not None:
        own, beside = lax.optimization_barrier((own, beside))
    result = jnp.zeros((SIDE,) + block.shape, block.dtype)
    pieces = {step: partner(block, sizes, leg, step) for step in STEPS[1:]}
    pieces[0] = own
    for step in STEPS:
        result = lax.dynamic_update_slice(
            result, pieces[step][None], (spots[step],) + (jnp.uint32(0),) * block.ndim
        )
    return result.reshape((-1,) + block.shape[1:]), beside


def scatter_blocks(values, sizes, leg, spots):
    values = values.reshape((SIDE, -1) + values.shape[1:])
    pieces = []
    for step in STEPS:
        start = (spots[step],) + (jnp.uint32(0),) * (values.ndim - 1)
        piece = lax.dynamic_slice(values, start, (1,) + values.shape[1:])[0]
        pieces.append(partner(piece, sizes, leg, step) if step else piece)
    return pieces


def total(pieces):
    result = pieces[0].astype(jnp.float32)
    for piece in pieces[1:]:
        result = result + piece.astype(jnp.float32)
    return result.astype(jnp.bfloat16)


def rounded(value):
    return value.astype(jnp.bfloat16).astype(jnp.float32)


def pack_kernel(weight_ref, hidden_ref, ids_ref, probs_ref, out_ref):
    probs = probs_ref[...]
    own_rows, kept = probs.shape
    width = hidden_ref.shape[1]
    row = lax.broadcasted_iota(jnp.int32, (own_rows, 1), 0)
    weight = jnp.zeros((own_rows, 1), jnp.float32)
    for i in range(own_rows):
        weight = jnp.where(row == i, weight_ref[i], weight)
    ids = ids_ref[...]
    high = ((ids >> 9) - ID_SHIFT).astype(jnp.float32)
    low = ((ids & (DIGIT - 1)) - HALF).astype(jnp.float32)
    weighted = probs * weight
    weighted_high = rounded(weighted)
    mass = jnp.sum(probs, axis=1, keepdims=True) * weight
    column = lax.broadcasted_iota(jnp.int32, (own_rows, 2 * kept), 1)
    pieces = jnp.zeros((own_rows, 2 * kept), jnp.float32)
    for i in range(3):
        part = rounded(mass)
        pieces = jnp.where(column == i, part, pieces)
        mass = mass - part
    tail = jnp.concatenate(
        [
            jnp.concatenate([high, low], axis=1),
            jnp.concatenate([weighted_high, rounded(weighted - weighted_high)], axis=1),
            pieces,
        ],
        axis=1,
    ).astype(jnp.bfloat16)
    hidden = hidden_ref[...]
    for i in range(out_ref.shape[0]):
        out_ref[i, :, :width] = hidden
        out_ref[i, :, width:] = tail


def pack(hidden, ids, probs, weight, copies):
    own_rows, width = hidden.shape
    kept = ids.shape[1]
    vmem = pl.BlockSpec(memory_space=pltpu.VMEM)
    return pl.pallas_call(
        pack_kernel,
        out_shape=jax.ShapeDtypeStruct((copies, own_rows, width + 6 * kept), jnp.bfloat16),
        in_specs=[pl.BlockSpec(memory_space=pltpu.SMEM), vmem, vmem, vmem],
        out_specs=vmem,
        name="pack",
    )(weight, hidden, ids, probs)


def target_kernel(first_ref, digits_ref, probs_ref, out_ref, place_ref):
    entries = out_ref.shape[0] // 2
    kept = place_ref.shape[0]
    digits = digits_ref[...].astype(jnp.float32).T.astype(jnp.int32)
    probs = probs_ref[...].astype(jnp.float32).T
    probs = probs[:kept] + probs[kept:]
    ids = (digits[:kept] + ID_SHIFT) * DIGIT + digits[kept:] + HALF
    own = ids - first_ref[0]
    other = ids - first_ref[1]
    none = jnp.int32(4 * entries)
    place = jnp.where((other >= 0) & (other < entries), other + entries, none)
    place = jnp.where((own >= 0) & (own < entries), own, place)
    rows = out_ref.shape[1]
    step = 16
    index = lax.broadcasted_iota(jnp.int32, (step, rows), 0)

    def take(place):
        chosen = jnp.min(place, axis=0, keepdims=True)
        hit = place == chosen
        amount = jnp.sum(jnp.where(hit, probs, 0.0), axis=0, keepdims=True)
        return chosen, amount, jnp.where(hit, none, place)

    def put(place, fresh):
        chosen, amount, place = take(place)
        second, second_amount, place = take(place)
        place_ref[...] = place

        def one(i, carry):
            at = pl.ds(pl.multiple_of(i * step, step), step)
            here = index + i * step
            value = jnp.zeros((step, rows), jnp.float32) if fresh else out_ref[at]
            value = jnp.where(here == chosen, amount, value)
            out_ref[at] = jnp.where(here == second, second_amount, value)
            return carry

        lax.fori_loop(0, 2 * entries // step, one, 0, unroll=2)
        return jnp.min(place)

    lax.while_loop(
        lambda lowest: lowest < none, lambda lowest: put(place_ref[...], False), put(place, True)
    )


def dense_target(gathered, firsts, width, kept, entries):
    rows = gathered.shape[0]
    at = width // (2 * kept)
    return pl.pallas_call(
        target_kernel,
        out_shape=jax.ShapeDtypeStruct((2 * entries, rows), jnp.float32),
        grid=(1,),
        in_specs=[
            pl.BlockSpec(memory_space=pltpu.SMEM),
            pl.BlockSpec((rows, 2 * kept), lambda i: (0, at)),
            pl.BlockSpec((rows, 2 * kept), lambda i: (0, at + 1)),
        ],
        out_specs=pl.BlockSpec((2 * entries, rows), lambda i: (0, 0)),
        scratch_shapes=[pltpu.VMEM((kept, rows), jnp.int32)],
        cost_estimate=pl.CostEstimate(flops=10000000, bytes_accessed=4000000, transcendentals=0),
        compiler_params=pltpu.CompilerParams(vmem_limit_bytes=8 * 1024 * 1024),
        name="target",
    )(firsts, gathered, gathered)


def logits_kernel(gathered_ref, weights_ref, exp_ref, stats_ref):
    width = weights_ref.shape[1]
    tile = 1024
    dims = (((1,), (1,)), ((), ()))
    for start in range(0, width, tile):
        at = slice(start, start + tile)
        part = lax.dot_general(
            weights_ref[:, at], gathered_ref[:, at], dims, preferred_element_type=jnp.float32
        )
        exp_ref[...] = part if start == 0 else exp_ref[...] + part
    logits = exp_ref[...]
    top = jnp.max(logits, axis=0, keepdims=True)
    exponent = jnp.exp(logits - top)
    exp_ref[...] = exponent
    stats_ref[0:1] = top
    stats_ref[1:2] = jnp.sum(exponent, axis=0, keepdims=True)


def exponents(gathered, weights):
    rows = gathered.shape[0]
    entries, width = weights.shape
    vmem = pl.BlockSpec(memory_space=pltpu.VMEM)
    return pl.pallas_call(
        logits_kernel,
        out_shape=(
            jax.ShapeDtypeStruct((entries, rows), jnp.float32),
            jax.ShapeDtypeStruct((2, rows), jnp.float32),
        ),
        in_specs=[vmem] * 2,
        out_specs=(vmem, vmem),
        compiler_params=pltpu.CompilerParams(vmem_limit_bytes=24 * 1024 * 1024),
        cost_estimate=pl.CostEstimate(
            flops=2 * entries * rows * width,
            bytes_accessed=2 * entries * width,
            transcendentals=entries * rows,
        ),
        name="exponents",
    )(gathered, weights)


def grad_kernel(
    stats_ref, local_ref, gathered_ref, exp_ref, target_ref, weights_ref,
    out_ref, own_grad_ref, other_grad_ref,
):
    entries, width = weights_ref.shape
    tile = 512
    tops = stats_ref[:, 0, :]
    top = jnp.max(tops, axis=0, keepdims=True)
    total = jnp.sum(stats_ref[:, 1, :] * jnp.exp(tops - top), axis=0, keepdims=True)
    tail = gathered_ref[:, gathered_ref.shape[1] - 128 :]
    mass = jnp.sum(tail.astype(jnp.float32).T, axis=0, keepdims=True)
    scale = mass * jnp.exp(local_ref[0:1] - top) / total
    grad = (exp_ref[...] * scale - target_ref[...]).astype(jnp.bfloat16)
    own_grad_ref[...] = grad[: entries // 2]
    other_grad_ref[...] = grad[entries // 2 :]
    turned = grad.T
    for start in range(0, width, tile):
        at = slice(start, start + tile)
        out = jnp.dot(turned, weights_ref[:, at], preferred_element_type=jnp.float32)
        out_ref[:, at] = out.astype(jnp.bfloat16)


def gradients(stats, local, gathered, exponent, target, weights):
    entries, width = weights.shape
    rows = gathered.shape[0]
    vmem = pl.BlockSpec(memory_space=pltpu.VMEM)
    return pl.pallas_call(
        grad_kernel,
        out_shape=(
            jax.ShapeDtypeStruct((rows, width), jnp.bfloat16),
            jax.ShapeDtypeStruct((entries // 2, rows), jnp.bfloat16),
            jax.ShapeDtypeStruct((entries // 2, rows), jnp.bfloat16),
        ),
        in_specs=[vmem] * 6,
        out_specs=(vmem,) * 3,
        compiler_params=pltpu.CompilerParams(vmem_limit_bytes=28 * 1024 * 1024),
        cost_estimate=pl.CostEstimate(
            flops=2 * entries * rows * width,
            bytes_accessed=2 * entries * width,
            transcendentals=0,
        ),
        name="gradients",
    )(stats, local, gathered, exponent, target, weights)


def per_device(sizes, hidden_states, head_weight, teacher_ids, teacher_probs, row_weight):
    size_y, size_z, size_x, _ = sizes
    own_rows, width = hidden_states.shape
    entries = head_weight.shape[0]
    kept = teacher_ids.shape[1]
    group = size_z * own_rows
    rows = size_y * size_x * group
    core = lax.axis_index("core")
    device = lax.axis_index(AXES)
    place_x, place_y = lax.axis_index("x"), lax.axis_index("y")
    first_place = jnp.where(core == 0, place_x, place_y).astype(jnp.uint32)
    second_place = jnp.where(core == 0, place_y, place_x).astype(jnp.uint32)
    first_spots = [first_place ^ step for step in range(SIDE)]
    second_spots = [second_place ^ step for step in range(SIDE)]
    firsts = jnp.stack([device * entries, (device + 1 - 2 * core) * entries])
    other_weight = lax.ppermute(head_weight, "core", SWAP)

    with jax.named_scope("pack"):
        hidden_states, first_spots, second_spots, firsts = lax.optimization_barrier(
            (hidden_states, first_spots, second_spots, firsts)
        )
        packed = pack(hidden_states, teacher_ids, teacher_probs, row_weight, size_z)

    with jax.named_scope("gather"):
        across_z = lax.all_to_all(packed, "z", 0, 0, tiled=True).reshape(group, -1)
        gathered, _ = gather_blocks(across_z, sizes, 0, first_spots)
        gathered, other_weight = lax.optimization_barrier((gathered, other_weight))
        weights = jnp.concatenate([head_weight, other_weight], axis=0)
        gathered, weights = gather_blocks(gathered, sizes, 1, second_spots, weights)
        hidden = gathered[:, :width]

    with jax.named_scope("target"):
        target = dense_target(gathered, firsts, width, kept, entries)

    with jax.named_scope("logits"):
        exponent, local = exponents(gathered, weights)

    with jax.named_scope("stats"):
        local, target = lax.optimization_barrier((local, target))
        stats = spread(local, ("y", "z", "x"), size_y * size_z * size_x)
        stats = stats.reshape(-1, 2, rows)

    with jax.named_scope("grads"):
        partial, grad, other_grad = gradients(
            stats, local, gathered, exponent, target, weights
        )

    with jax.named_scope("scatter"):
        partial, other_grad = lax.optimization_barrier((partial, other_grad))
        pieces = scatter_blocks(partial, sizes, 1, second_spots)

    with jax.named_scope("grad_weight"):
        other_part = jnp.dot(other_grad, hidden, preferred_element_type=jnp.float32)
        other_part = other_part.astype(jnp.bfloat16)
        returned = lax.ppermute(other_part, "core", SWAP)

    with jax.named_scope("scatter"):
        pieces[0], other_part = lax.optimization_barrier((pieces[0], other_part))
        summed = total(pieces)
        summed, grad = lax.optimization_barrier((summed, grad))
        pieces = scatter_blocks(summed, sizes, 0, first_spots)

    with jax.named_scope("grad_weight"):
        own_part = jnp.dot(grad, hidden, preferred_element_type=jnp.float32)
        grad_weight = (own_part + returned.astype(jnp.float32)).astype(jnp.bfloat16)

    with jax.named_scope("scatter"):
        pieces[0], grad_weight = lax.optimization_barrier((pieces[0], grad_weight))
        summed = total(pieces).reshape(size_z, own_rows, width)
        pieces = lax.all_to_all(summed, "z", 0, 0, tiled=True)
        grad_hidden = jnp.sum(pieces.astype(jnp.float32), axis=0).astype(jnp.bfloat16)
    return grad_hidden, grad_weight


def solution(mesh):
    sizes = (4, 8, 4, 2)
    grid = Mesh(mesh.devices.reshape(sizes), AXES)
    in_specs = (P(AXES, None), P(AXES, None), P(AXES, None), P(AXES, None), P(AXES))
    out_specs = (P(AXES, None), P(AXES, None))

    def body(*args):
        return per_device(sizes, *args)

    return jax.shard_map(
        body, mesh=grid, in_specs=in_specs, out_specs=out_specs, check_vma=False
    )
```

```python
import jax
import jax.numpy as jnp
import numpy as np
from jax import lax
from jax.experimental import pallas as pl
from jax.experimental.pallas import tpu as pltpu
from jax.sharding import Mesh, PartitionSpec as P

AXES = ("y", "z", "x", "core")
SWAP = [(0, 1), (1, 0)]
SIDE = 4
STEPS = (0, 2, 1, 3)
DIGIT = 512
HALF = 256
ID_SHIFT = 148


def spread(block, axes, count):
    copies = jnp.broadcast_to(block[None], (count,) + block.shape)
    return lax.all_to_all(copies, axes, 0, 0, tiled=True)


def partner(block, sizes, leg, step):
    pairs = []
    for source, (y, z, x, core) in enumerate(np.ndindex(*sizes)):
        if (core + leg) % 2 == 0:
            x = x ^ step
        else:
            y = y ^ step
        pairs.append((source, int(np.ravel_multi_index((y, z, x, core), sizes))))
    return lax.ppermute(block, AXES, pairs)


def gather_blocks(block, sizes, leg, spots, beside=None):
    own = block
    if beside is not None:
        own, beside = lax.optimization_barrier((own, beside))
    result = jnp.zeros((SIDE,) + block.shape, block.dtype)
    pieces = {step: partner(block, sizes, leg, step) for step in STEPS[1:]}
    pieces[0] = own
    for step in STEPS:
        result = lax.dynamic_update_slice(
            result, pieces[step][None], (spots[step],) + (jnp.uint32(0),) * block.ndim
        )
    return result.reshape((-1,) + block.shape[1:]), beside


def scatter_blocks(values, sizes, leg, spots):
    values = values.reshape((SIDE, -1) + values.shape[1:])
    pieces = []
    for step in STEPS:
        start = (spots[step],) + (jnp.uint32(0),) * (values.ndim - 1)
        piece = lax.dynamic_slice(values, start, (1,) + values.shape[1:])[0]
        pieces.append(partner(piece, sizes, leg, step) if step else piece)
    return pieces


def total(pieces):
    result = pieces[0].astype(jnp.float32)
    for piece in pieces[1:]:
        result = lax.optimization_barrier(result) + piece.astype(jnp.float32)
    return result.astype(jnp.bfloat16)


def rounded(value):
    return value.astype(jnp.bfloat16).astype(jnp.float32)


def pack_kernel(weight_ref, hidden_ref, ids_ref, probs_ref, out_ref):
    probs = probs_ref[...]
    own_rows, kept = probs.shape
    width = hidden_ref.shape[1]
    row = lax.broadcasted_iota(jnp.int32, (own_rows, 1), 0)
    weight = jnp.zeros((own_rows, 1), jnp.float32)
    for i in range(own_rows):
        weight = jnp.where(row == i, weight_ref[i], weight)
    ids = ids_ref[...]
    high = ((ids >> 9) - ID_SHIFT).astype(jnp.float32)
    low = ((ids & (DIGIT - 1)) - HALF).astype(jnp.float32)
    weighted = probs * weight
    weighted_high = rounded(weighted)
    mass = jnp.sum(probs, axis=1, keepdims=True) * weight
    column = lax.broadcasted_iota(jnp.int32, (own_rows, 2 * kept), 1)
    pieces = jnp.zeros((own_rows, 2 * kept), jnp.float32)
    for i in range(3):
        part = rounded(mass)
        pieces = jnp.where(column == i, part, pieces)
        mass = mass - part
    tail = jnp.concatenate(
        [
            jnp.concatenate([high, low], axis=1),
            jnp.concatenate([weighted_high, rounded(weighted - weighted_high)], axis=1),
            pieces,
        ],
        axis=1,
    ).astype(jnp.bfloat16)
    hidden = hidden_ref[...]
    for i in range(out_ref.shape[0]):
        out_ref[i, :, :width] = hidden
        out_ref[i, :, width:] = tail


def pack(hidden, ids, probs, weight, copies):
    own_rows, width = hidden.shape
    kept = ids.shape[1]
    vmem = pl.BlockSpec(memory_space=pltpu.VMEM)
    return pl.pallas_call(
        pack_kernel,
        out_shape=jax.ShapeDtypeStruct((copies, own_rows, width + 6 * kept), jnp.bfloat16),
        in_specs=[pl.BlockSpec(memory_space=pltpu.SMEM), vmem, vmem, vmem],
        out_specs=vmem,
        name="pack",
    )(weight, hidden, ids, probs)


def target_kernel(first_ref, digits_ref, probs_ref, out_ref, place_ref):
    entries = out_ref.shape[0] // 2
    kept = place_ref.shape[0]
    digits = digits_ref[...].astype(jnp.float32).T.astype(jnp.int32)
    probs = probs_ref[...].astype(jnp.float32).T
    probs = probs[:kept] + probs[kept:]
    ids = (digits[:kept] + ID_SHIFT) * DIGIT + digits[kept:] + HALF
    own = ids - first_ref[0]
    other = ids - first_ref[1]
    none = jnp.int32(4 * entries)
    place = jnp.where((other >= 0) & (other < entries), other + entries, none)
    place = jnp.where((own >= 0) & (own < entries), own, place)
    rows = out_ref.shape[1]
    step = 16
    index = lax.broadcasted_iota(jnp.int32, (step, rows), 0)

    def take(place):
        chosen = jnp.min(place, axis=0, keepdims=True)
        hit = place == chosen
        amount = jnp.sum(jnp.where(hit, probs, 0.0), axis=0, keepdims=True)
        return chosen, amount, jnp.where(hit, none, place)

    def put(place, fresh):
        chosen, amount, place = take(place)
        second, second_amount, place = take(place)
        place_ref[...] = place

        def one(i, carry):
            at = pl.ds(pl.multiple_of(i * step, step), step)
            here = index + i * step
            value = jnp.zeros((step, rows), jnp.float32) if fresh else out_ref[at]
            value = jnp.where(here == chosen, amount, value)
            out_ref[at] = jnp.where(here == second, second_amount, value)
            return carry

        lax.fori_loop(0, 2 * entries // step, one, 0, unroll=2)
        return jnp.min(place)

    lax.while_loop(
        lambda lowest: lowest < none, lambda lowest: put(place_ref[...], False), put(place, True)
    )


def dense_target(gathered, firsts, width, kept, entries):
    rows = gathered.shape[0]
    at = width // (2 * kept)
    return pl.pallas_call(
        target_kernel,
        out_shape=jax.ShapeDtypeStruct((2 * entries, rows), jnp.float32),
        grid=(1,),
        in_specs=[
            pl.BlockSpec(memory_space=pltpu.SMEM),
            pl.BlockSpec((rows, 2 * kept), lambda i: (0, at)),
            pl.BlockSpec((rows, 2 * kept), lambda i: (0, at + 1)),
        ],
        out_specs=pl.BlockSpec((2 * entries, rows), lambda i: (0, 0)),
        scratch_shapes=[pltpu.VMEM((kept, rows), jnp.int32)],
        cost_estimate=pl.CostEstimate(flops=10000000, bytes_accessed=4000000, transcendentals=0),
        compiler_params=pltpu.CompilerParams(vmem_limit_bytes=8 * 1024 * 1024),
        name="target",
    )(firsts, gathered, gathered)


def logits_kernel(gathered_ref, weights_ref, exp_ref, stats_ref):
    width = weights_ref.shape[1]
    tile = 1024
    dims = (((1,), (1,)), ((), ()))
    for start in range(0, width, tile):
        at = slice(start, start + tile)
        part = lax.dot_general(
            weights_ref[:, at], gathered_ref[:, at], dims, preferred_element_type=jnp.float32
        )
        exp_ref[...] = part if start == 0 else exp_ref[...] + part
    logits = exp_ref[...]
    top = jnp.max(logits, axis=0, keepdims=True)
    exponent = jnp.exp(logits - top)
    exp_ref[...] = exponent
    total = jnp.sum(exponent, axis=0, keepdims=True)
    lanes = stats_ref.shape[1]
    half = stats_ref.shape[0] // 2
    for i in range(half):
        at = slice(i * lanes, (i + 1) * lanes)
        stats_ref[i : i + 1] = top[:, at]
        stats_ref[half + i : half + i + 1] = total[:, at]


def exponents(gathered, weights):
    rows = gathered.shape[0]
    entries, width = weights.shape
    vmem = pl.BlockSpec(memory_space=pltpu.VMEM)
    return pl.pallas_call(
        logits_kernel,
        out_shape=(
            jax.ShapeDtypeStruct((entries, rows), jnp.float32),
            jax.ShapeDtypeStruct((2 * rows // 128, 128), jnp.float32),
        ),
        in_specs=[vmem] * 2,
        out_specs=(vmem, vmem),
        compiler_params=pltpu.CompilerParams(vmem_limit_bytes=24 * 1024 * 1024),
        cost_estimate=pl.CostEstimate(
            flops=2 * entries * rows * width,
            bytes_accessed=2 * entries * width,
            transcendentals=entries * rows,
        ),
        name="exponents",
    )(gathered, weights)


def grad_kernel(
    stats_ref, local_ref, gathered_ref, exp_ref, target_ref, weights_ref,
    out_ref, own_grad_ref, other_grad_ref,
):
    entries, width = weights_ref.shape
    tile = 512
    half = stats_ref.shape[1] // 2
    tops, totals, locals_ = [], [], []
    for i in range(half):
        values = stats_ref[:, i, :]
        top = jnp.max(values, axis=0, keepdims=True)
        total = stats_ref[:, half + i, :] * jnp.exp(values - top)
        tops.append(top)
        totals.append(jnp.sum(total, axis=0, keepdims=True))
        locals_.append(local_ref[i : i + 1])
    top = jnp.concatenate(tops, axis=1)
    total = jnp.concatenate(totals, axis=1)
    local = jnp.concatenate(locals_, axis=1)
    tail = gathered_ref[:, gathered_ref.shape[1] - 128 :]
    mass = jnp.sum(tail.astype(jnp.float32).T, axis=0, keepdims=True)
    scale = mass * jnp.exp(local - top) / total
    grad = (exp_ref[...] * scale - target_ref[...]).astype(jnp.bfloat16)
    own_grad_ref[...] = grad[: entries // 2]
    other_grad_ref[...] = grad[entries // 2 :]
    turned = grad.T
    for start in range(0, width, tile):
        at = slice(start, start + tile)
        out = jnp.dot(turned, weights_ref[:, at], preferred_element_type=jnp.float32)
        out_ref[:, at] = out.astype(jnp.bfloat16)


def gradients(stats, local, gathered, exponent, target, weights):
    entries, width = weights.shape
    rows = gathered.shape[0]
    vmem = pl.BlockSpec(memory_space=pltpu.VMEM)
    return pl.pallas_call(
        grad_kernel,
        out_shape=(
            jax.ShapeDtypeStruct((rows, width), jnp.bfloat16),
            jax.ShapeDtypeStruct((entries // 2, rows), jnp.bfloat16),
            jax.ShapeDtypeStruct((entries // 2, rows), jnp.bfloat16),
        ),
        in_specs=[vmem] * 6,
        out_specs=(vmem,) * 3,
        compiler_params=pltpu.CompilerParams(vmem_limit_bytes=28 * 1024 * 1024),
        cost_estimate=pl.CostEstimate(
            flops=2 * entries * rows * width,
            bytes_accessed=2 * entries * width,
            transcendentals=0,
        ),
        name="gradients",
    )(stats, local, gathered, exponent, target, weights)


def product_kernel(own_grad_ref, other_grad_ref, own_ref, other_ref, out_ref):
    out = jnp.dot(own_grad_ref[...], own_ref[...], preferred_element_type=jnp.float32)
    out += jnp.dot(other_grad_ref[...], other_ref[...], preferred_element_type=jnp.float32)
    out_ref[...] = out.astype(jnp.bfloat16)


def product(own_grad, other_grad, own_hidden, other_hidden, width):
    entries, rows = own_grad.shape
    tile = 1024
    grad_spec = pl.BlockSpec((entries, rows), lambda n: (0, 0))
    hidden_spec = pl.BlockSpec((rows, tile), lambda n: (0, n))
    return pl.pallas_call(
        product_kernel,
        out_shape=jax.ShapeDtypeStruct((entries, width), jnp.bfloat16),
        grid=(width // tile,),
        in_specs=[grad_spec, grad_spec, hidden_spec, hidden_spec],
        out_specs=pl.BlockSpec((entries, tile), lambda n: (0, n)),
        compiler_params=pltpu.CompilerParams(vmem_limit_bytes=16 * 1024 * 1024),
        cost_estimate=pl.CostEstimate(
            flops=4 * entries * rows * width,
            bytes_accessed=2 * entries * width + 4 * rows * width,
            transcendentals=0,
        ),
        name="product",
    )(own_grad, other_grad, own_hidden, other_hidden)


def per_device(sizes, hidden_states, head_weight, teacher_ids, teacher_probs, row_weight):
    size_y, size_z, size_x, _ = sizes
    own_rows, width = hidden_states.shape
    entries = head_weight.shape[0]
    kept = teacher_ids.shape[1]
    group = size_z * own_rows
    rows = size_y * size_x * group
    core = lax.axis_index("core")
    device = lax.axis_index(AXES)
    place_x, place_y = lax.axis_index("x"), lax.axis_index("y")
    first_place = jnp.where(core == 0, place_x, place_y).astype(jnp.uint32)
    second_place = jnp.where(core == 0, place_y, place_x).astype(jnp.uint32)
    first_spots = [first_place ^ step for step in range(SIDE)]
    second_spots = [second_place ^ step for step in range(SIDE)]
    firsts = jnp.stack([device * entries, (device + 1 - 2 * core) * entries])
    other_weight = lax.ppermute(head_weight, "core", SWAP)

    with jax.named_scope("pack"):
        hidden_states, first_spots, second_spots, firsts = lax.optimization_barrier(
            (hidden_states, first_spots, second_spots, firsts)
        )
        packed = pack(hidden_states, teacher_ids, teacher_probs, row_weight, size_z)

    with jax.named_scope("gather"):
        across_z = lax.all_to_all(packed, "z", 0, 0, tiled=True).reshape(group, -1)
        gathered, _ = gather_blocks(across_z, sizes, 0, first_spots)
        gathered, other_weight = lax.optimization_barrier((gathered, other_weight))
        weights = jnp.concatenate([head_weight, other_weight], axis=0)
        gathered, weights = gather_blocks(gathered, sizes, 1, second_spots, weights)

    with jax.named_scope("target"):
        target = dense_target(gathered, firsts, width, kept, entries)

    with jax.named_scope("logits"):
        exponent, local = exponents(gathered, weights)

    with jax.named_scope("stats"):
        local, target = lax.optimization_barrier((local, target))
        stats = spread(local, ("y", "z", "x"), size_y * size_z * size_x)
        stats = stats.reshape((-1,) + local.shape)
        stats, sent = lax.optimization_barrier((stats, gathered))
        other_gathered = lax.ppermute(sent, "core", SWAP)

    with jax.named_scope("grads"):
        partial, grad, other_grad = gradients(
            stats, local, gathered, exponent, target, weights
        )

    with jax.named_scope("scatter"):
        pieces = scatter_blocks(partial, sizes, 1, second_spots)

    with jax.named_scope("grad_weight"):
        received = lax.ppermute(other_grad, "core", SWAP)
        grad_weight = product(grad, received, gathered, other_gathered, width)

    with jax.named_scope("scatter"):
        pieces[0], grad_weight = lax.optimization_barrier((pieces[0], grad_weight))
        summed = total(pieces)
        pieces = scatter_blocks(summed, sizes, 0, first_spots)
        summed = total(pieces).reshape(size_z, own_rows, width)
        pieces = lax.all_to_all(summed, "z", 0, 0, tiled=True)
        grad_hidden = jnp.sum(pieces.astype(jnp.float32), axis=0).astype(jnp.bfloat16)

    return grad_hidden, grad_weight


def solution(mesh):
    sizes = (4, 8, 4, 2)
    grid = Mesh(mesh.devices.reshape(sizes), AXES)
    in_specs = (P(AXES, None), P(AXES, None), P(AXES, None), P(AXES, None), P(AXES))
    out_specs = (P(AXES, None), P(AXES, None))

    def body(*args):
        return per_device(sizes, *args)

    return jax.shard_map(
        body, mesh=grid, in_specs=in_specs, out_specs=out_specs, check_vma=False
    )
```

```python
import jax
import jax.numpy as jnp
import numpy as np
from jax import lax
from jax.experimental import pallas as pl
from jax.experimental.pallas import tpu as pltpu
from jax.sharding import Mesh, PartitionSpec as P

AXES = ("y", "z", "x", "core")
SWAP = [(0, 1), (1, 0)]
SIDE = 4
STEPS = (0, 2, 1, 3)
DIGIT = 512
HALF = 256
ID_SHIFT = 148


def spread(block, axes, count):
    copies = jnp.broadcast_to(block[None], (count,) + block.shape)
    return lax.all_to_all(copies, axes, 0, 0, tiled=True)


def partner(block, sizes, leg, step):
    pairs = []
    for source, (y, z, x, core) in enumerate(np.ndindex(*sizes)):
        if (core + leg) % 2 == 0:
            x = x ^ step
        else:
            y = y ^ step
        pairs.append((source, int(np.ravel_multi_index((y, z, x, core), sizes))))
    return lax.ppermute(block, AXES, pairs)


def gather_blocks(block, sizes, leg, spots, beside=None):
    own = block
    if beside is not None:
        own, beside = lax.optimization_barrier((own, beside))
    result = jnp.zeros((SIDE,) + block.shape, block.dtype)
    pieces = {step: partner(block, sizes, leg, step) for step in STEPS[1:]}
    pieces[0] = own
    for step in STEPS:
        result = lax.dynamic_update_slice(
            result, pieces[step][None], (spots[step],) + (jnp.uint32(0),) * block.ndim
        )
    return result.reshape((-1,) + block.shape[1:]), beside


def scatter_blocks(values, sizes, leg, spots):
    values = values.reshape((SIDE, -1) + values.shape[1:])
    pieces = []
    for step in STEPS:
        start = (spots[step],) + (jnp.uint32(0),) * (values.ndim - 1)
        piece = lax.dynamic_slice(values, start, (1,) + values.shape[1:])[0]
        pieces.append(partner(piece, sizes, leg, step) if step else piece)
    return pieces


def total(pieces):
    result = pieces[0].astype(jnp.float32)
    for piece in pieces[1:]:
        result = lax.optimization_barrier(result) + piece.astype(jnp.float32)
    return result.astype(jnp.bfloat16)


def rounded(value):
    return value.astype(jnp.bfloat16).astype(jnp.float32)


def pack_kernel(weight_ref, hidden_ref, ids_ref, probs_ref, out_ref):
    probs = probs_ref[...]
    own_rows, kept = probs.shape
    width = hidden_ref.shape[1]
    row = lax.broadcasted_iota(jnp.int32, (own_rows, 1), 0)
    weight = jnp.zeros((own_rows, 1), jnp.float32)
    for i in range(own_rows):
        weight = jnp.where(row == i, weight_ref[i], weight)
    ids = ids_ref[...]
    high = ((ids >> 9) - ID_SHIFT).astype(jnp.float32)
    low = ((ids & (DIGIT - 1)) - HALF).astype(jnp.float32)
    weighted = probs * weight
    weighted_high = rounded(weighted)
    mass = jnp.sum(probs, axis=1, keepdims=True) * weight
    column = lax.broadcasted_iota(jnp.int32, (own_rows, 2 * kept), 1)
    pieces = jnp.zeros((own_rows, 2 * kept), jnp.float32)
    for i in range(3):
        part = rounded(mass)
        pieces = jnp.where(column == i, part, pieces)
        mass = mass - part
    tail = jnp.concatenate(
        [
            jnp.concatenate([high, low], axis=1),
            jnp.concatenate([weighted_high, rounded(weighted - weighted_high)], axis=1),
            pieces,
        ],
        axis=1,
    ).astype(jnp.bfloat16)
    hidden = hidden_ref[...]
    for i in range(out_ref.shape[0]):
        out_ref[i, :, :width] = hidden
        out_ref[i, :, width:] = tail


def pack(hidden, ids, probs, weight, copies):
    own_rows, width = hidden.shape
    kept = ids.shape[1]
    vmem = pl.BlockSpec(memory_space=pltpu.VMEM)
    return pl.pallas_call(
        pack_kernel,
        out_shape=jax.ShapeDtypeStruct((copies, own_rows, width + 6 * kept), jnp.bfloat16),
        in_specs=[pl.BlockSpec(memory_space=pltpu.SMEM), vmem, vmem, vmem],
        out_specs=vmem,
        name="pack",
    )(weight, hidden, ids, probs)


def target_kernel(first_ref, digits_ref, probs_ref, out_ref, place_ref):
    entries = out_ref.shape[0] // 2
    kept = place_ref.shape[0]
    digits = digits_ref[...].astype(jnp.float32).T.astype(jnp.int32)
    probs = probs_ref[...].astype(jnp.float32).T
    probs = probs[:kept] + probs[kept:]
    ids = (digits[:kept] + ID_SHIFT) * DIGIT + digits[kept:] + HALF
    own = ids - first_ref[0]
    other = ids - first_ref[1]
    none = jnp.int32(4 * entries)
    place = jnp.where((other >= 0) & (other < entries), other + entries, none)
    place = jnp.where((own >= 0) & (own < entries), own, place)
    rows = out_ref.shape[1]
    step = 16
    index = lax.broadcasted_iota(jnp.int32, (step, rows), 0)

    def take(place):
        chosen = jnp.min(place, axis=0, keepdims=True)
        hit = place == chosen
        amount = jnp.sum(jnp.where(hit, probs, 0.0), axis=0, keepdims=True)
        return chosen, amount, jnp.where(hit, none, place)

    def put(place, fresh):
        chosen, amount, place = take(place)
        second, second_amount, place = take(place)
        place_ref[...] = place

        def one(i, carry):
            at = pl.ds(pl.multiple_of(i * step, step), step)
            here = index + i * step
            value = jnp.zeros((step, rows), jnp.float32) if fresh else out_ref[at]
            value = jnp.where(here == chosen, amount, value)
            out_ref[at] = jnp.where(here == second, second_amount, value)
            return carry

        lax.fori_loop(0, 2 * entries // step, one, 0, unroll=37)
        return jnp.min(place)

    lax.while_loop(
        lambda lowest: lowest < none, lambda lowest: put(place_ref[...], False), put(place, True)
    )


def dense_target(gathered, firsts, width, kept, entries):
    rows = gathered.shape[0]
    at = width // (2 * kept)
    return pl.pallas_call(
        target_kernel,
        out_shape=jax.ShapeDtypeStruct((2 * entries, rows), jnp.float32),
        grid=(1,),
        in_specs=[
            pl.BlockSpec(memory_space=pltpu.SMEM),
            pl.BlockSpec((rows, 2 * kept), lambda i: (0, at)),
            pl.BlockSpec((rows, 2 * kept), lambda i: (0, at + 1)),
        ],
        out_specs=pl.BlockSpec((2 * entries, rows), lambda i: (0, 0)),
        scratch_shapes=[pltpu.VMEM((kept, rows), jnp.int32)],
        cost_estimate=pl.CostEstimate(flops=10000000, bytes_accessed=4000000, transcendentals=0),
        compiler_params=pltpu.CompilerParams(vmem_limit_bytes=8 * 1024 * 1024),
        name="target",
    )(firsts, gathered, gathered)


def logits_kernel(gathered_ref, weights_ref, exp_ref, stats_ref):
    width = weights_ref.shape[1]
    tile = 1024
    dims = (((1,), (1,)), ((), ()))
    for start in range(0, width, tile):
        at = slice(start, start + tile)
        part = lax.dot_general(
            weights_ref[:, at], gathered_ref[:, at], dims, preferred_element_type=jnp.float32
        )
        exp_ref[...] = part if start == 0 else exp_ref[...] + part
    logits = exp_ref[...]
    top = jnp.max(logits, axis=0, keepdims=True)
    exponent = jnp.exp(logits - top)
    exp_ref[...] = exponent
    total = jnp.sum(exponent, axis=0, keepdims=True)
    lanes = stats_ref.shape[1]
    half = stats_ref.shape[0] // 2
    for i in range(half):
        at = slice(i * lanes, (i + 1) * lanes)
        stats_ref[i : i + 1] = top[:, at]
        stats_ref[half + i : half + i + 1] = total[:, at]


def exponents(gathered, weights):
    rows = gathered.shape[0]
    entries, width = weights.shape
    vmem = pl.BlockSpec(memory_space=pltpu.VMEM)
    return pl.pallas_call(
        logits_kernel,
        out_shape=(
            jax.ShapeDtypeStruct((entries, rows), jnp.float32),
            jax.ShapeDtypeStruct((2 * rows // 128, 128), jnp.float32),
        ),
        in_specs=[vmem] * 2,
        out_specs=(vmem, vmem),
        compiler_params=pltpu.CompilerParams(vmem_limit_bytes=24 * 1024 * 1024),
        cost_estimate=pl.CostEstimate(
            flops=2 * entries * rows * width,
            bytes_accessed=2 * entries * width,
            transcendentals=entries * rows,
        ),
        name="exponents",
    )(gathered, weights)


def grad_kernel(
    stats_ref, local_ref, gathered_ref, exp_ref, target_ref, weights_ref,
    out_ref, own_grad_ref, other_grad_ref,
):
    entries, width = weights_ref.shape
    tile = 512
    half = stats_ref.shape[1] // 2
    tops, totals, locals_ = [], [], []
    for i in range(half):
        values = stats_ref[:, i, :]
        top = jnp.max(values, axis=0, keepdims=True)
        total = stats_ref[:, half + i, :] * jnp.exp(values - top)
        tops.append(top)
        totals.append(jnp.sum(total, axis=0, keepdims=True))
        locals_.append(local_ref[i : i + 1])
    top = jnp.concatenate(tops, axis=1)
    total = jnp.concatenate(totals, axis=1)
    local = jnp.concatenate(locals_, axis=1)
    tail = gathered_ref[:, gathered_ref.shape[1] - 128 :]
    mass = jnp.sum(tail.astype(jnp.float32).T, axis=0, keepdims=True)
    scale = mass * jnp.exp(local - top) / total
    grad = (exp_ref[...] * scale - target_ref[...]).astype(jnp.bfloat16)
    own_grad_ref[...] = grad[: entries // 2]
    other_grad_ref[...] = grad[entries // 2 :]
    turned = grad.T
    for start in range(0, width, tile):
        at = slice(start, start + tile)
        out = jnp.dot(turned, weights_ref[:, at], preferred_element_type=jnp.float32)
        out_ref[:, at] = out.astype(jnp.bfloat16)


def gradients(stats, local, gathered, exponent, target, weights):
    entries, width = weights.shape
    rows = gathered.shape[0]
    vmem = pl.BlockSpec(memory_space=pltpu.VMEM)
    return pl.pallas_call(
        grad_kernel,
        out_shape=(
            jax.ShapeDtypeStruct((rows, width), jnp.bfloat16),
            jax.ShapeDtypeStruct((entries // 2, rows), jnp.bfloat16),
            jax.ShapeDtypeStruct((entries // 2, rows), jnp.bfloat16),
        ),
        in_specs=[vmem] * 6,
        out_specs=(vmem,) * 3,
        compiler_params=pltpu.CompilerParams(vmem_limit_bytes=28 * 1024 * 1024),
        cost_estimate=pl.CostEstimate(
            flops=2 * entries * rows * width,
            bytes_accessed=2 * entries * width,
            transcendentals=0,
        ),
        name="gradients",
    )(stats, local, gathered, exponent, target, weights)


def product_kernel(own_grad_ref, other_grad_ref, own_ref, other_ref, out_ref):
    out = jnp.dot(own_grad_ref[...], own_ref[...], preferred_element_type=jnp.float32)
    out += jnp.dot(other_grad_ref[...], other_ref[...], preferred_element_type=jnp.float32)
    out_ref[...] = out.astype(jnp.bfloat16)


def product(own_grad, other_grad, own_hidden, other_hidden, width):
    entries, rows = own_grad.shape
    tile = 1024
    grad_spec = pl.BlockSpec((entries, rows), lambda n: (0, 0))
    hidden_spec = pl.BlockSpec((rows, tile), lambda n: (0, n))
    return pl.pallas_call(
        product_kernel,
        out_shape=jax.ShapeDtypeStruct((entries, width), jnp.bfloat16),
        grid=(width // tile,),
        in_specs=[grad_spec, grad_spec, hidden_spec, hidden_spec],
        out_specs=pl.BlockSpec((entries, tile), lambda n: (0, n)),
        compiler_params=pltpu.CompilerParams(vmem_limit_bytes=16 * 1024 * 1024),
        cost_estimate=pl.CostEstimate(
            flops=4 * entries * rows * width,
            bytes_accessed=2 * entries * width + 4 * rows * width,
            transcendentals=0,
        ),
        name="product",
    )(own_grad, other_grad, own_hidden, other_hidden)


def per_device(sizes, hidden_states, head_weight, teacher_ids, teacher_probs, row_weight):
    size_y, size_z, size_x, _ = sizes
    own_rows, width = hidden_states.shape
    entries = head_weight.shape[0]
    kept = teacher_ids.shape[1]
    group = size_z * own_rows
    rows = size_y * size_x * group
    core = lax.axis_index("core")
    device = lax.axis_index(AXES)
    place_x, place_y = lax.axis_index("x"), lax.axis_index("y")
    first_place = jnp.where(core == 0, place_x, place_y).astype(jnp.uint32)
    second_place = jnp.where(core == 0, place_y, place_x).astype(jnp.uint32)
    first_spots = [first_place ^ step for step in range(SIDE)]
    second_spots = [second_place ^ step for step in range(SIDE)]
    firsts = jnp.stack([device * entries, (device + 1 - 2 * core) * entries])

    with jax.named_scope("pack"):
        hidden_states, first_spots, second_spots, firsts = lax.optimization_barrier(
            (hidden_states, first_spots, second_spots, firsts)
        )
        packed = pack(hidden_states, teacher_ids, teacher_probs, row_weight, size_z)
        packed, own_weight = lax.optimization_barrier((packed, head_weight))
        other_weight = lax.ppermute(own_weight, "core", SWAP)

    with jax.named_scope("gather"):
        across_z = lax.all_to_all(packed, "z", 0, 0, tiled=True).reshape(group, -1)
        gathered, _ = gather_blocks(across_z, sizes, 0, first_spots)
        weights = jnp.concatenate([head_weight, other_weight], axis=0)
        gathered, weights = gather_blocks(gathered, sizes, 1, second_spots, weights)

    with jax.named_scope("target"):
        target = dense_target(gathered, firsts, width, kept, entries)

    with jax.named_scope("logits"):
        exponent, local = exponents(gathered, weights)

    with jax.named_scope("stats"):
        local, target = lax.optimization_barrier((local, target))
        stats = spread(local, ("y", "z", "x"), size_y * size_z * size_x)
        stats = stats.reshape((-1,) + local.shape)
        stats, sent = lax.optimization_barrier((stats, gathered))
        other_gathered = lax.ppermute(sent, "core", SWAP)

    with jax.named_scope("grads"):
        partial, grad, other_grad = gradients(
            stats, local, gathered, exponent, target, weights
        )

    with jax.named_scope("scatter"):
        pieces = scatter_blocks(partial, sizes, 1, second_spots)

    with jax.named_scope("grad_weight"):
        received = lax.ppermute(other_grad, "core", SWAP)
        grad_weight = product(grad, received, gathered, other_gathered, width)

    with jax.named_scope("scatter"):
        pieces[0], grad_weight = lax.optimization_barrier((pieces[0], grad_weight))
        summed = total(pieces)
        pieces = scatter_blocks(summed, sizes, 0, first_spots)
        summed = total(pieces).reshape(size_z, own_rows, width)
        pieces = lax.all_to_all(summed, "z", 0, 0, tiled=True)
        grad_hidden = jnp.sum(pieces.astype(jnp.float32), axis=0).astype(jnp.bfloat16)

    return grad_hidden, grad_weight


def solution(mesh):
    sizes = (4, 8, 4, 2)
    grid = Mesh(mesh.devices.reshape(sizes), AXES)
    in_specs = (P(AXES, None), P(AXES, None), P(AXES, None), P(AXES, None), P(AXES))
    out_specs = (P(AXES, None), P(AXES, None))

    def body(*args):
        return per_device(sizes, *args)

    return jax.shard_map(
        body, mesh=grid, in_specs=in_specs, out_specs=out_specs, check_vma=False
    )
```
